1024 devices in a mesh: dp: 64 (over z, x), row: 4 (over y_hi, core), col: 4 (over y_lo).
Axes of the slice: x: 8, y: 8 (y_hi: 2, y_lo: 4; y = y_hi * 4 + y_lo), z: 8, core: 2. Of those that a mesh axis runs over, the one named last changes fastest.
Arguments:
- attn_mix: bfloat16 [98304, 8192], P(('dp', 'col'), 'row'), may hold values from -24 to 24
- value_weight: bfloat16 [8192, 1024], P('row', 'col'), may hold values from -0.0625 to 0.0625
- readout: bfloat16 [98304, 1024], P(('dp', 'row'), 'col'), may hold values from -0.0390625 to 0.0390625
- ref_scores: float32 [384, 2], replicated, may hold values from -6 to 6
- domain_label: int32 [384, 1], replicated, may hold values from 0 to 15
- prior_weights: float32 [16], replicated, may hold values from 0.01 to 0.1
Outputs:
- grad_weight: float32 [8192, 1024], P(('row', 'dp'), 'col')
- new_weights: float32 [16], replicated
The draws below stay inside these ranges and needn't reach their ends.
Inputs may be any that keep to these rules, and one draw needn't show every extreme that they name: `domain_label`: every domain labels at least one pair.
All inputs are finite; a program needn't handle non-finite values.
Results may differ from the reference program's by a relative error of at most 0.0029.
Values may be sent and summed in bfloat16 or wider, within the bound.
A program may use at most 32 MiB of HBM per device.

```python
import math
import jax
import jax.numpy as jnp
from jax import lax

D = 8192
KVDIM = 1024
DOMAINS = 16
SEQ = 128
ALL_PAIRS = 384
TOKENS = 98304


def with_spikes(values, rng, source, target, shards_of, factor):
    owner, partner = [(jnp.arange(values.shape[dim]) // (values.shape[dim] // shards_of)).reshape([-1 if axis == dim else 1 for axis in range(values.ndim)]) for dim in (source, target)]
    chosen = jax.random.permutation(rng, shards_of)[partner]
    strong = (owner == chosen) | (owner == (partner + shards_of // 2) % shards_of)
    return jnp.where(strong, factor * values, values)


def levels(stream_key, dims, cuts, least, largest):
    gain = 1.0
    for axis_at, parts in cuts:
        steps = jax.random.uniform(jax.random.fold_in(jax.random.fold_in(stream_key, 6), axis_at), (parts,), jnp.float32, least / len(cuts), largest / len(cuts))
        gain = gain * jnp.repeat(jnp.exp(steps), dims[axis_at] // parts).reshape((-1,) + (1,) * (len(dims) - 1 - axis_at))
    return gain


def distinct(stream_key, rows, amount, top, lift):
    ranking = jax.random.permutation(jax.random.fold_in(stream_key, 1), amount)
    pull = ranking
    for power in range(3):
        pull = pull * pull // amount
    pull = pull * lift // amount
    tickets = jax.random.randint(jax.random.fold_in(stream_key, 2), (rows, amount), 0, 4096) + pull
    holders = jax.random.permutation(jax.random.fold_in(stream_key, 3), rows)[jnp.arange(amount) % rows]
    tickets = jnp.where(jnp.arange(rows)[:, None] == holders[None, :], 1 << 14, tickets)
    score = tickets * amount + jnp.arange(amount)
    return lax.top_k(score.astype(jnp.int32), top)[1].astype(jnp.int32)


def noise(rng, shape, spread, bound, cuts=(), kind=jnp.bfloat16):
    values = jax.random.normal(rng, shape, jnp.float32) * spread
    if len(cuts) > 0:
        values = levels(rng, shape, cuts, -0.22, 0.18) * values
    return jnp.clip(values, min=-bound, max=bound).astype(kind)


def noise_with(key, extent, scale, most, cuts, heavy, kind=jnp.bfloat16):
    drawn = scale * jax.random.normal(key, extent, jnp.float32)
    if cuts:
        drawn = drawn * levels(key, extent, cuts, -0.22, 0.18)
    return jnp.clip(with_spikes(drawn, jax.random.fold_in(key, 3), *heavy), -most, most).astype(kind)


def setup_inputs(seed: int = 0) -> dict:
    streams_of = jax.random.split(jax.random.key(seed), 7)
    return {
        "attn_mix": noise_with(streams_of[0], (TOKENS, D), 1.0, 24.0, ((0, 256), (1, 4)), (0, 1, 256, 6.0)),
        "value_weight": noise(streams_of[1], (D, KVDIM), D ** -0.5, 0.0625, ((0, 4), (1, 4))),
        "readout": noise(streams_of[2], (TOKENS, KVDIM), ((SEQ * KVDIM) ** -0.5), 0.0390625, ((0, 256), (1, 4))),
        "ref_scores": noise(streams_of[3], (ALL_PAIRS, 2), 1.0, 6.0, (), jnp.float32),
        "domain_label": distinct(streams_of[4], ALL_PAIRS, DOMAINS, 1, 512),
        "prior_weights": jnp.clip(jnp.exp(jax.random.uniform(streams_of[5], (DOMAINS,), jnp.float32, math.log(0.01), math.log(0.1))), 0.01, 0.1),
    }


def reference(attn_mix, value_weight, readout, ref_scores, domain_label, prior_weights):
    values = jnp.dot(attn_mix, value_weight, preferred_element_type=jnp.float32)
    per_token = jnp.sum(values * readout.astype(jnp.float32), axis=1)
    scores = per_token.reshape(ALL_PAIRS, 2, SEQ).sum(axis=2)
    margin = (scores[:, 0] - ref_scores[:, 0]) - (scores[:, 1] - ref_scores[:, 1])
    pair_loss = jax.nn.softplus(-margin)
    labels = domain_label[:, 0]
    onehot = (labels[:, None] == jnp.arange(DOMAINS, dtype=jnp.int32)[None, :]).astype(jnp.float32)
    counts = jnp.sum(onehot, axis=0)
    domain_loss = jnp.sum(onehot * pair_loss[:, None], axis=0) / counts
    raised = prior_weights * jnp.exp(domain_loss)
    new_weights = raised / jnp.sum(raised)
    per_domain = new_weights / counts
    coeff = ALL_PAIRS * jax.nn.sigmoid(-margin) * jnp.sum(onehot * per_domain[None, :], axis=1)
    signed = coeff[:, None] * jnp.array([-1.0, 1.0], dtype=jnp.float32)[None, :]
    tok_coef = jnp.broadcast_to(signed[:, :, None], (ALL_PAIRS, 2, SEQ)).reshape(TOKENS)
    token_grad = (tok_coef[:, None] * readout.astype(jnp.float32)).astype(jnp.bfloat16)
    grad_weight = lax.dot_general(attn_mix, token_grad, (((0,), (0,)), ((), ())), preferred_element_type=jnp.float32)
    return grad_weight, new_weights
```

```python
import functools

import jax
import jax.numpy as jnp
from jax import lax
from jax.experimental import pallas as pl
from jax.experimental.pallas import tpu as pltpu
from jax.sharding import PartitionSpec as P

DOMAINS = 16
SEQ = 128
PARTS = 4
MESH = pl.DeviceIdType.MESH


def kernel(
    nz, nx, nr, nc,
    x_ref, w_ref, r_ref, ref_ref, label_ref, prior_ref,
    grad_ref, weights_ref,
    wbuf, rbuf, xt, tg, line, rowx, rowz, stage, got, send2, got2, sum3, got3,
    wy_s, wy_r, w1_s, w1_r, w2_s, w2_r, r_s, r_r,
    l_s, l_r, x_s, x_r, z_s, z_r, p1_s, p1_r, p2_s, p2_r, p3_s, p3_r,
):
    tb, feat = x_ref.shape
    ob = w_ref.shape[1]
    fb = feat // (nz * nx)
    sb = nc * ob // PARTS
    resp = tb // SEQ
    pairs_grp = nc * resp // 2
    all_pairs = label_ref.shape[1]
    per_col = ob // sb
    f32 = jnp.float32

    dp, row, col = lax.axis_index("dp"), lax.axis_index("row"), lax.axis_index("col")
    z, x = dp // nx, dp % nx
    me = row * nc + col
    nline = nr * nc

    def at_line(k):
        idx = lax.rem(me + k, nline)
        return (dp, idx // nc, idx % nc)

    def at_x(k):
        return (z * nx + lax.rem(x + k, nx), row, col)

    def at_z(k):
        return (lax.rem(z + k, nz) * nx + x, row, col)

    def at_col(k):
        return (dp, row, lax.rem(col + k, nc))

    def send(src, dst, ssem, rsem, dev):
        copy = pltpu.make_async_remote_copy(
            src_ref=src, dst_ref=dst, send_sem=ssem, recv_sem=rsem,
            device_id=dev, device_id_type=MESH,
        )
        copy.start()
        return copy

    sent = []
    axes = ((x, nx, at_x), (z, nz, at_z))

    barrier = pltpu.get_barrier_semaphore()
    for k in range(1, nline):
        pl.semaphore_signal(barrier, inc=1, device_id=at_line(k), device_id_type=MESH)
    for _, n, at in axes:
        for k in range(1, n):
            pl.semaphore_signal(barrier, inc=1, device_id=at(k), device_id_type=MESH)
    pl.semaphore_wait(barrier, nline - 1 + nx - 1 + nz - 1)

    rows = pl.ds(pl.multiple_of(dp * fb, fb), fb)
    wy = []
    for k in range(1, nc):
        slot = nc - k - 1
        wy.append(send(w_ref.at[rows, :], wbuf.at[slot, z, x], wy_s.at[k], wy_r.at[slot], at_col(k)))

    reads = []
    for k in range(1, nr):
        reads.append(send(r_ref, rbuf.at[col], r_s.at[k], r_r.at[col], (dp, lax.rem(row + k, nr), row)))
    own_read = pltpu.make_async_copy(r_ref, rbuf.at[col], r_r.at[col])
    far_read = pltpu.make_async_remote_copy(
        src_ref=r_ref, dst_ref=rbuf.at[col], send_sem=r_s.at[0], recv_sem=r_r.at[col],
        device_id=(dp, row, row), device_id_type=MESH,
    )

    @pl.when(row == col)
    def _():
        own_read.start()

    @pl.when(row != col)
    def _():
        far_read.start()

    lanes = (pl.ds(0, ob // 2), pl.ds(ob // 2, ob // 2))
    w1 = [[], []]
    if nc > 1:
        for slot in range(nc - 1):
            pltpu.make_async_copy(wbuf.at[slot, z, x], wbuf.at[slot, z, x], wy_r.at[slot]).wait()
        for k in range(1, max(nx, nz)):
            for h, (_, n, at) in enumerate(axes):
                if k < n:
                    block = wbuf.at[:, z, x, :, lanes[h]]
                    w1[h].append(send(block, block, w1_s.at[h, k], w1_r.at[h, k], at(k)))

    for b in range(nz):
        block = x_ref[:, b * nx * fb:(b + 1) * nx * fb]
        xt[b] = jnp.swapaxes(block, 0, 1).reshape(nx, fb, tb)
    lane = lax.broadcasted_iota(jnp.int32, (1, all_pairs), 1)
    onehot = (label_ref[...] == lax.broadcasted_iota(jnp.int32, (DOMAINS, all_pairs), 0)).astype(f32)
    counts = jnp.sum(onehot, axis=1, keepdims=True)

    if nc > 1:
        for h in range(2):
            for copy in w1[h]:
                copy.wait_recv()
        chains = []
        for h in range(2):
            pos, n, at = axes[1 - h]
            for d, (sign, length) in enumerate(((1, n // 2), (-1, n - 1 - n // 2))):
                for slot in range(nc - 1):
                    chains.append((h, d, slot, pos, n, at, sign, length))
        moving = {}
        for s in range(max(nx, nz) // 2 + 1):
            for h, d, slot, pos, n, at, sign, length in chains:
                if 0 < s <= length:
                    moving[h, d, slot, s - 1].wait_recv()
                if s < length:
                    src = lax.rem(pos - sign * s + n, n)
                    if h == 0:
                        block = wbuf.at[slot, src, :, :, lanes[h]]
                    else:
                        block = wbuf.at[slot, :, src, :, lanes[h]]
                    moving[h, d, slot, s] = send(
                        block, block, w2_s.at[h, d, slot, s], w2_r.at[h, d, slot, s], at(sign % n)
                    )
        sent += wy + w1[0] + w1[1] + list(moving.values())

    for j in range(nc):
        pltpu.make_async_copy(rbuf.at[j], rbuf.at[j], r_r.at[j]).wait()
    sums = [jnp.zeros((1, ob), f32) for _ in range(resp)]
    for k in range(nc):
        weight = w_ref[...] if k == 0 else wbuf[k - 1].reshape(feat, ob)
        values = jnp.dot(x_ref[...], weight, preferred_element_type=f32)
        prod = values * rbuf[lax.rem(col + k, nc)].astype(f32)
        for q in range(resp):
            sums[q] = sums[q] + jnp.sum(prod[q * SEQ:(q + 1) * SEQ], axis=0, keepdims=True)
    mine = jnp.zeros((1, all_pairs), f32)
    for q in range(resp):
        which = col * resp + q
        score = jnp.sum(sums[q], axis=1, keepdims=True)
        sign = jnp.where(which % 2 == 0, 1.0, -1.0).astype(f32)
        mine = mine + jnp.where(lane == dp * pairs_grp + which // 2, sign * score, 0.0)

    def exchange(buf, pos, n, at, ssem, rsem, value):
        buf[pos] = value
        copies = [send(buf.at[pos], buf.at[pos], ssem.at[k], rsem.at[k], at(k)) for k in range(1, n)]
        for copy in copies:
            copy.wait_recv()
        total = buf[0]
        for i in range(1, n):
            total = total + buf[i]
        sent.extend(copies)
        return total

    mine = exchange(line, me, nline, at_line, l_s, l_r, mine)
    mine = exchange(rowx, x, nx, at_x, x_s, x_r, mine)
    mine = exchange(rowz, z, nz, at_z, z_s, z_r, mine)
    margin = mine - (ref_ref[0:1, :] - ref_ref[1:2, :])
    loss = jnp.maximum(-margin, 0.0) + jnp.log1p(jnp.exp(-jnp.abs(margin)))
    domain_loss = jnp.sum(onehot * loss, axis=1, keepdims=True) / counts
    eye = lax.broadcasted_iota(jnp.int32, (DOMAINS, DOMAINS), 0) == lax.broadcasted_iota(
        jnp.int32, (DOMAINS, DOMAINS), 1
    )
    prior = jnp.sum(jnp.where(eye, prior_ref[...], 0.0), axis=1, keepdims=True)
    raised = prior * jnp.exp(domain_loss)
    new_weights = raised / jnp.sum(raised, axis=0, keepdims=True)
    weights_ref[...] = jnp.sum(jnp.where(eye, new_weights, 0.0), axis=0, keepdims=True)
    coeff = (
        all_pairs * jax.nn.sigmoid(-margin)
        * jnp.sum(onehot * (new_weights / counts), axis=0, keepdims=True)
    )
    for q in range(resp):
        which = col * resp + q
        own = jnp.sum(
            jnp.where(lane == dp * pairs_grp + which // 2, coeff, 0.0), axis=1, keepdims=True
        )
        own = own * jnp.where(which % 2 == 0, -1.0, 1.0).astype(f32)
        for j in range(PARTS):
            at_lane = (j % per_col) * sb
            block = rbuf[j // per_col, q * SEQ:(q + 1) * SEQ, at_lane:at_lane + sb]
            tg[j, q * SEQ:(q + 1) * SEQ, :] = (own * block.astype(f32)).astype(jnp.bfloat16)

    def part(h, target, j):
        lhs = xt[:, target] if h == 0 else xt[target]
        lhs = lhs.reshape(lhs.shape[0] * fb, tb)
        return jnp.dot(lhs, tg[2 * h + j], preferred_element_type=f32)

    chains = []
    for h in range(2):
        pos, n, at = axes[h]
        for j in range(2):
            long = n // 2
            lengths = (long, n - 1 - long) if j == 0 else (n - 1 - long, long)
            for d in range(2):
                chains.append((h, d, j, pos, n, at, 1 - 2 * d, lengths[d]))
    moving = {}
    for s in range(max(nx, nz) // 2):
        for h, d, j, pos, n, at, sign, length in chains:
            if s < length:
                chunk = part(h, lax.rem(pos + sign * (length - s) + n, n), j)
                if s > 0:
                    moving[h, d, j, s - 1].wait_recv()
                    chunk = chunk + got[h, d, j, s - 1].astype(f32)
                stage[h, d, j, s] = chunk.astype(jnp.bfloat16)
                moving[h, d, j, s] = send(
                    stage.at[h, d, j, s], got.at[h, d, j, s],
                    p1_s.at[h, d, j, s], p1_r.at[h, d, j, s], at(sign % n),
                )
    for h in range(2):
        pos, n, at = axes[h]
        for j in range(2):
            chunk = part(h, pos, j)
            for ch in chains:
                if ch[0] == h and ch[2] == j and ch[7] > 0:
                    last = ch[7] - 1
                    moving[h, ch[1], j, last].wait_recv()
                    chunk = chunk + got[h, ch[1], j, last].astype(f32)
            send2[h, :, j] = chunk.reshape(chunk.shape[0] // fb, fb, sb)
    sent += list(moving.values())

    second = []
    for h in range(2):
        pos, n, at = axes[1 - h]
        for k in range(1, n):
            second.append(send(
                send2.at[h, lax.rem(pos + k, n)], got2.at[h, pos], p2_s.at[h, k], p2_r.at[h, k], at(k)
            ))
    for copy in second:
        copy.wait_recv()
    sent += second
    for h in range(2):
        pos, n, at = axes[1 - h]
        total = send2[h, pos]
        for k in range(1, n):
            total = total + got2[h, lax.rem(pos - k + n, n)]
        sum3[2 * h:2 * h + 2] = total

    third = []
    for k in range(1, nc):
        target = lax.rem(col + k, nc)
        third.append(send(
            sum3.at[pl.ds(target * per_col, per_col)], got3.at[col], p3_s.at[k], p3_r.at[k], at_col(k)
        ))
    for copy in third:
        copy.wait_recv()
    sent += third
    for i in range(per_col):
        total = sum3[col * per_col + i]
        for k in range(1, nc):
            total = total + got3[lax.rem(col - k + nc, nc), i]
        grad_ref[:, i * sb:(i + 1) * sb] = total

    for copy in reads + sent:
        copy.wait_send()

    @pl.when(row != col)
    def _():
        far_read.wait_send()


def local(nz, nx, nr, nc, attn_mix, value_weight, readout, ref_scores, domain_label, prior_weights):
    tb, feat = attn_mix.shape
    ob = value_weight.shape[1]
    fb = feat // (nz * nx)
    sb = nc * ob // PARTS
    all_pairs = domain_label.shape[0]
    ring = max(nz, nx)
    vmem = pl.BlockSpec(memory_space=pltpu.VMEM)
    bf16, f32 = jnp.bfloat16, jnp.float32
    dma = pltpu.SemaphoreType.DMA
    assert nz == nx
    grad, weights = pl.pallas_call(
        functools.partial(kernel, nz, nx, nr, nc),
        out_shape=(
            jax.ShapeDtypeStruct((fb, ob), f32),
            jax.ShapeDtypeStruct((1, DOMAINS), f32),
        ),
        in_specs=[vmem] * 6,
        out_specs=(vmem, vmem),
        scratch_shapes=[
            pltpu.VMEM((max(nc - 1, 1), nz, nx, fb, ob), bf16),
            pltpu.VMEM((nc, tb, ob), bf16),
            pltpu.VMEM((nz, nx, fb, tb), bf16),
            pltpu.VMEM((PARTS, tb, sb), bf16),
            pltpu.VMEM((nr * nc, 1, all_pairs), f32),
            pltpu.VMEM((nx, 1, all_pairs), f32),
            pltpu.VMEM((nz, 1, all_pairs), f32),
            pltpu.VMEM((2, 2, 2, ring // 2, ring * fb, sb), bf16),
            pltpu.VMEM((2, 2, 2, ring // 2, ring * fb, sb), bf16),
            pltpu.VMEM((2, ring, 2, fb, sb), f32),
            pltpu.VMEM((2, ring, 2, fb, sb), f32),
            pltpu.VMEM((PARTS, fb, sb), f32),
            pltpu.VMEM((nc, ob // sb, fb, sb), f32),
            dma((nc,)), dma((nc,)),
            dma((2, ring)), dma((2, ring)),
            dma((2, 2, max(nc - 1, 1), ring // 2)), dma((2, 2, max(nc - 1, 1), ring // 2)),
            dma((nr,)), dma((nc,)),
            dma((nr * nc,)), dma((nr * nc,)),
            dma((nx,)), dma((nx,)),
            dma((nz,)), dma((nz,)),
            dma((2, 2, 2, ring // 2)), dma((2, 2, 2, ring // 2)),
            dma((2, ring)), dma((2, ring)),
            dma((nc,)), dma((nc,)),
        ],
        compiler_params=pltpu.CompilerParams(
            collective_id=0, has_side_effects=True, vmem_limit_bytes=48 * 1024 * 1024
        ),
        cost_estimate=pl.CostEstimate(
            flops=4 * tb * feat * nc * ob, bytes_accessed=4 * tb * feat, transcendentals=0
        ),
    )(attn_mix, value_weight, readout, ref_scores.T, domain_label.T, prior_weights.reshape(1, DOMAINS))
    return grad, weights.reshape(DOMAINS)


def build(mesh, nz, nx):
    placed = (P(("dp", "col"), "row"), P("row", "col"), P(("dp", "row"), "col"), P(), P(), P())
    return jax.shard_map(
        functools.partial(local, nz, nx, mesh.shape["row"], mesh.shape["col"]),
        mesh=mesh, in_specs=placed, out_specs=(P(("row", "dp"), "col"), P()), check_vma=False,
    )


def solution(mesh):
    return build(mesh, 8, mesh.shape["dp"] // 8)
```

```python
import functools

import jax
import jax.numpy as jnp
from jax import lax
from jax.experimental import pallas as pl
from jax.experimental.pallas import tpu as pltpu
from jax.sharding import PartitionSpec as P

DOMAINS = 16
SEQ = 128
PARTS = 4
CUTS = 2
FAR = 3
MESH = pl.DeviceIdType.MESH


def kernel(
    nz, nx, nr, nc,
    x_hbm, w_hbm, r_hbm, ref_hbm, label_hbm, prior_hbm,
    grad_ref, weights_ref,
    x_ref, w_ref, r_ref, ref_ref, label_ref, prior_ref,
    wbuf, rbuf, xt, tg, rowc, rowy, rowx, rowz, stage, got, send2, got2, far2, gotfar2, sum3, got3,
    in_s, wy_s, wy_r, w2_s, w2_r, r_s, r_r, f_s,
    c_s, c_r, y_s, y_r, x_s, x_r, z_s, z_r, p1_s, p1_r, p2_s, p2_r, p3_s, p3_r,
):
    tb, feat = x_ref.shape
    ob = w_ref.shape[-1]
    fb = feat // (nz * nx)
    sb = nc * ob // PARTS
    resp = tb // SEQ
    pairs_grp = nc * resp // 2
    all_pairs = label_ref.shape[1]
    per_col = ob // sb
    f32 = jnp.float32

    dp, row, col = lax.axis_index("dp"), lax.axis_index("row"), lax.axis_index("col")
    z, x = dp // nx, dp % nx
    cores = 2 if nr % 2 == 0 else 1
    y_high, core = row // cores, row % cores
    y, ny = y_high * nc + col, nr // cores * nc

    def at_core(k):
        return (dp, y_high * cores + lax.rem(core + k, cores), col)

    def at_y(k):
        other = lax.rem(y + k, ny)
        return (dp, other // nc * cores + core, other % nc)

    def at_x(k):
        return (z * nx + lax.rem(x + k, nx), row, col)

    def at_z(k):
        return (lax.rem(z + k, nz) * nx + x, row, col)

    def at_col(k):
        return (dp, row, lax.rem(col + k, nc))

    def send(src, dst, ssem, rsem, dev):
        copy = pltpu.make_async_remote_copy(
            src_ref=src, dst_ref=dst, send_sem=ssem, recv_sem=rsem,
            device_id=dev, device_id_type=MESH,
        )
        copy.start()
        return copy

    sent = []
    axes = ((x, nx, at_x), (z, nz, at_z))

    loads = []
    for i, (src, dst) in enumerate((
        (w_hbm, w_ref), (r_hbm, r_ref), (x_hbm, x_ref),
        (label_hbm, label_ref), (ref_hbm, ref_ref), (prior_hbm, prior_ref),
    )):
        loads.append(pltpu.make_async_copy(src, dst, in_s.at[i]))
        loads[i].start()

    barrier = pltpu.get_barrier_semaphore()
    count = 0
    for n, at in ((cores, at_core), (ny, at_y), (nx, at_x), (nz, at_z)):
        for k in range(1, n):
            pl.semaphore_signal(barrier, inc=1, device_id=at(k), device_id_type=MESH)
            count += 1
    loads[0].wait()
    loads[1].wait()
    pl.semaphore_wait(barrier, count)

    lanes = (pl.ds(0, ob // 2), pl.ds(ob // 2, ob // 2))

    def w_block(ref, h, i):
        return ref.at[i, :, :, lanes[h]] if h == 0 else ref.at[:, i, :, lanes[h]]

    wy = []
    for k in range(1, nc):
        slot = nc - k - 1
        for h, i in enumerate((z, x)):
            wy.append(send(
                w_block(w_ref, h, i), w_block(wbuf.at[slot], h, i),
                wy_s.at[h, k], wy_r.at[h, slot], at_col(k),
            ))

    reads = []
    for k in range(1, nr // cores):
        there = lax.rem(y_high + k, nr // cores) * cores + core
        reads.append(send(r_ref, rbuf.at[col], r_s.at[k], r_r.at[col], (dp, there, row)))
    own_read = pltpu.make_async_copy(r_ref, rbuf.at[col], r_r.at[col])
    far_read = pltpu.make_async_remote_copy(
        src_ref=r_ref, dst_ref=rbuf.at[col], send_sem=r_s.at[0], recv_sem=r_r.at[col],
        device_id=(dp, row, row), device_id_type=MESH,
    )

    @pl.when(row == col)
    def _():
        own_read.start()

    @pl.when(row != col)
    def _():
        far_read.start()

    for load in loads[2:]:
        load.wait()
    for b in range(nz):
        block = x_ref[:, b * nx * fb:(b + 1) * nx * fb]
        xt[b] = jnp.swapaxes(block, 0, 1).reshape(nx, fb, tb)
    lane = lax.broadcasted_iota(jnp.int32, (1, all_pairs), 1)
    onehot = (label_ref[...] == lax.broadcasted_iota(jnp.int32, (DOMAINS, all_pairs), 0)).astype(f32)
    counts = jnp.sum(onehot, axis=1, keepdims=True)

    chains, moving = [], {}
    for slot in range(nc - 1):
        for h in range(2):
            pos, n, at = axes[1 - h]
            for d, sign in enumerate((1, -1)):
                length = n // 2 if (h + slot + d) % 2 == 0 else n - 1 - n // 2
                chains.append((h, d, slot, pos, n, at, sign, length))

    def spread(s):
        for h, d, slot, pos, n, at, sign, length in chains:
            if s == 0 and d == 0:
                block = w_block(wbuf.at[slot], h, pos)
                pltpu.make_async_copy(block, block, wy_r.at[h, slot]).wait()
            if 0 < s <= length:
                moving[h, d, slot, s - 1].wait_recv()
            if s < length:
                block = w_block(wbuf.at[slot], h, lax.rem(pos - sign * s + n, n))
                moving[h, d, slot, s] = send(
                    block, block, w2_s.at[h, d, slot, s], w2_r.at[h, d, slot, s], at(sign % n)
                )

    spread(0)

    passes = [
        pltpu.make_async_remote_copy(
            src_ref=rbuf.at[j], dst_ref=rbuf.at[j], send_sem=f_s.at[j], recv_sem=r_r.at[j],
            device_id=at_core(1), device_id_type=MESH,
        )
        for j in range(nc if cores > 1 else 0)
    ]
    passing = core == col % cores

    def pass_on():
        for j in range(nc):
            pltpu.make_async_copy(rbuf.at[j], rbuf.at[j], r_r.at[j]).wait()
            if cores > 1:
                @pl.when(passing)
                def _():
                    passes[j].start()

    steps = max(nx, nz) // 2
    for s in range(1, steps):
        spread(s)
    pass_on()
    spread(steps)
    sent += wy + list(moving.values())

    sums = [jnp.zeros((1, ob), f32) for _ in range(resp)]
    for k in range(nc):
        weight = (w_ref[...] if k == 0 else wbuf[k - 1]).reshape(feat, ob)
        values = jnp.dot(x_ref[...], weight, preferred_element_type=f32)
        prod = values * rbuf[lax.rem(col + k, nc)].astype(f32)
        for q in range(resp):
            sums[q] = sums[q] + jnp.sum(prod[q * SEQ:(q + 1) * SEQ], axis=0, keepdims=True)
    mine = jnp.zeros((1, all_pairs), f32)
    for q in range(resp):
        which = col * resp + q
        score = jnp.sum(sums[q], axis=1, keepdims=True)
        sign = jnp.where(which % 2 == 0, 1.0, -1.0).astype(f32)
        mine = mine + jnp.where(lane == dp * pairs_grp + which // 2, sign * score, 0.0)

    def exchange(buf, pos, n, at, ssem, rsem, value):
        buf[pos] = value
        copies = [send(buf.at[pos], buf.at[pos], ssem.at[k], rsem.at[k], at(k)) for k in range(1, n)]
        for copy in copies:
            copy.wait_recv()
        total = buf[0]
        for i in range(1, n):
            total = total + buf[i]
        sent.extend(copies)
        return total

    mine = exchange(rowc, core, cores, at_core, c_s, c_r, mine)
    mine = exchange(rowy, y, ny, at_y, y_s, y_r, mine)
    mine = exchange(rowx, x, nx, at_x, x_s, x_r, mine)
    mine = exchange(rowz, z, nz, at_z, z_s, z_r, mine)
    margin = mine - (ref_ref[0:1, :] - ref_ref[1:2, :])
    loss = jnp.maximum(-margin, 0.0) + jnp.log1p(jnp.exp(-jnp.abs(margin)))
    domain_loss = jnp.sum(onehot * loss, axis=1, keepdims=True) / counts
    eye = lax.broadcasted_iota(jnp.int32, (DOMAINS, DOMAINS), 0) == lax.broadcasted_iota(
        jnp.int32, (DOMAINS, DOMAINS), 1
    )
    prior = jnp.sum(jnp.where(eye, prior_ref[...], 0.0), axis=1, keepdims=True)
    raised = prior * jnp.exp(domain_loss)
    new_weights = raised / jnp.sum(raised, axis=0, keepdims=True)
    weights_ref[...] = jnp.sum(jnp.where(eye, new_weights, 0.0), axis=0, keepdims=True)
    coeff = (
        all_pairs * jax.nn.sigmoid(-margin)
        * jnp.sum(onehot * (new_weights / counts), axis=0, keepdims=True)
    )
    for q in range(resp):
        which = col * resp + q
        own = jnp.sum(
            jnp.where(lane == dp * pairs_grp + which // 2, coeff, 0.0), axis=1, keepdims=True
        )
        own = own * jnp.where(which % 2 == 0, -1.0, 1.0).astype(f32)
        for j in range(PARTS):
            at_lane = (j % per_col) * sb
            block = rbuf[j // per_col, q * SEQ:(q + 1) * SEQ, at_lane:at_lane + sb]
            tg[j, q * SEQ:(q + 1) * SEQ, :] = (own * block.astype(f32)).astype(jnp.bfloat16)

    def part(h, target, j):
        lhs = xt[:, target] if h == 0 else xt[target]
        lhs = lhs.reshape(lhs.shape[0] * fb, tb)
        return jnp.dot(lhs, tg[2 * h + j], preferred_element_type=f32)

    chains = []
    for j in range(2):
        for h in range(2):
            pos, n, at = axes[h]
            long = n // 2
            lengths = (long, n - 1 - long) if j == 0 else (n - 1 - long, long)
            for d in range(2):
                chains.append((h, d, j, pos, n, at, 1 - 2 * d, lengths[d]))
    moving = {}
    for s in range(max(nx, nz) // 2):
        for h, d, j, pos, n, at, sign, length in chains:
            if s < length:
                chunk = part(h, lax.rem(pos + sign * (length - s) + n, n), j)
                for u in range(CUTS):
                    piece = chunk[u * n * fb // CUTS:(u + 1) * n * fb // CUTS]
                    if s > 0:
                        moving[h, d, j, s - 1, u].wait_recv()
                        piece = piece + got[h, d, j, s - 1, u].astype(f32)
                    stage[h, d, j, s, u] = piece.astype(jnp.bfloat16)
                    moving[h, d, j, s, u] = send(
                        stage.at[h, d, j, s, u], got.at[h, d, j, s, u],
                        p1_s.at[h, d, j, s, u], p1_r.at[h, d, j, s, u], at(sign % n),
                    )
    for h in range(2):
        pos, n, at = axes[h]
        for j in range(2):
            chunk = part(h, pos, j)
            for ch in chains:
                if ch[0] == h and ch[2] == j and ch[7] > 0:
                    last = ch[7] - 1
                    for u in range(CUTS):
                        moving[h, ch[1], j, last, u].wait_recv()
                    chunk = chunk + got[h, ch[1], j, last].reshape(n * fb, sb).astype(f32)
            send2[h, :, j] = chunk.reshape(chunk.shape[0] // fb, fb, sb)
    sent += list(moving.values())

    second = []
    for h in range(2):
        pos, n, at = axes[1 - h]
        for k in sorted(range(1, n), key=lambda k: -min(k, n - k)):
            target, src, dst = lax.rem(pos + k, n), send2, got2
            if min(k, n - k) >= FAR:
                far2[h, target] = send2[h, target].astype(jnp.bfloat16)
                src, dst = far2, gotfar2
            second.append(send(
                src.at[h, target], dst.at[h, pos], p2_s.at[h, k], p2_r.at[h, k], at(k)
            ))
    for copy in second:
        copy.wait_recv()
    sent += second
    for h in range(2):
        pos, n, at = axes[1 - h]
        total = send2[h, pos]
        for k in range(1, n):
            there = gotfar2 if min(k, n - k) >= FAR else got2
            total = total + there[h, lax.rem(pos - k + n, n)].astype(f32)
        sum3[2 * h:2 * h + 2] = total

    third = []
    for k in range(1, nc):
        target = lax.rem(col + k, nc)
        third.append(send(
            sum3.at[pl.ds(target * per_col, per_col)], got3.at[col], p3_s.at[k], p3_r.at[k], at_col(k)
        ))
    for copy in third:
        copy.wait_recv()
    sent += third
    for i in range(per_col):
        total = sum3[col * per_col + i]
        for k in range(1, nc):
            total = total + got3[lax.rem(col - k + nc, nc), i]
        grad_ref[:, i * sb:(i + 1) * sb] = total

    for copy in reads + sent:
        copy.wait_send()

    @pl.when(row != col)
    def _():
        far_read.wait_send()

    if cores > 1:
        @pl.when(passing)
        def _():
            for copy in passes:
                copy.wait_send()


def local(nz, nx, nr, nc, attn_mix, value_weight, readout, ref_scores, domain_label, prior_weights):
    tb, feat = attn_mix.shape
    ob = value_weight.shape[1]
    fb = feat // (nz * nx)
    sb = nc * ob // PARTS
    all_pairs = domain_label.shape[0]
    ring = max(nz, nx)
    cores = 2 if nr % 2 == 0 else 1
    ny = nr // cores * nc
    vmem = pl.BlockSpec(memory_space=pltpu.VMEM)
    bf16, f32 = jnp.bfloat16, jnp.float32
    dma = pltpu.SemaphoreType.DMA
    assert nz == nx
    grad, weights = pl.pallas_call(
        functools.partial(kernel, nz, nx, nr, nc),
        out_shape=(
            jax.ShapeDtypeStruct((fb, ob), f32),
            jax.ShapeDtypeStruct((1, DOMAINS), f32),
        ),
        in_specs=[pl.BlockSpec(memory_space=pl.ANY)] * 6,
        out_specs=(vmem, vmem),
        scratch_shapes=[
            pltpu.VMEM(attn_mix.shape, bf16),
            pltpu.VMEM((nz, nx, fb, ob), bf16),
            pltpu.VMEM(readout.shape, bf16),
            pltpu.VMEM((2, all_pairs), f32),
            pltpu.VMEM((1, all_pairs), jnp.int32),
            pltpu.VMEM((1, DOMAINS), f32),
            pltpu.VMEM((max(nc - 1, 1), nz, nx, fb, ob), bf16),
            pltpu.VMEM((nc, tb, ob), bf16),
            pltpu.VMEM((nz, nx, fb, tb), bf16),
            pltpu.VMEM((PARTS, tb, sb), bf16),
            pltpu.VMEM((cores, 1, all_pairs), f32),
            pltpu.VMEM((ny, 1, all_pairs), f32),
            pltpu.VMEM((nx, 1, all_pairs), f32),
            pltpu.VMEM((nz, 1, all_pairs), f32),
            pltpu.VMEM((2, 2, 2, ring // 2, CUTS, ring * fb // CUTS, sb), bf16),
            pltpu.VMEM((2, 2, 2, ring // 2, CUTS, ring * fb // CUTS, sb), bf16),
            pltpu.VMEM((2, ring, 2, fb, sb), f32),
            pltpu.VMEM((2, ring, 2, fb, sb), f32),
            pltpu.VMEM((2, ring, 2, fb, sb), bf16),
            pltpu.VMEM((2, ring, 2, fb, sb), bf16),
            pltpu.VMEM((PARTS, fb, sb), f32),
            pltpu.VMEM((nc, ob // sb, fb, sb), f32),
            dma((6,)),
            dma((2, nc)), dma((2, nc)),
            dma((2, 2, max(nc - 1, 1), ring // 2)), dma((2, 2, max(nc - 1, 1), ring // 2)),
            dma((nr,)), dma((nc,)), dma((nc,)),
            dma((cores,)), dma((cores,)),
            dma((ny,)), dma((ny,)),
            dma((nx,)), dma((nx,)),
            dma((nz,)), dma((nz,)),
            dma((2, 2, 2, ring // 2, CUTS)), dma((2, 2, 2, ring // 2, CUTS)),
            dma((2, ring)), dma((2, ring)),
            dma((nc,)), dma((nc,)),
        ],
        compiler_params=pltpu.CompilerParams(
            collective_id=0, has_side_effects=True, vmem_limit_bytes=56 * 1024 * 1024
        ),
        cost_estimate=pl.CostEstimate(
            flops=4 * tb * feat * nc * ob, bytes_accessed=4 * tb * feat, transcendentals=0
        ),
    )(
        attn_mix, value_weight.reshape(nz, nx, fb, ob), readout,
        ref_scores.T, domain_label.T, prior_weights.reshape(1, DOMAINS),
    )
    return grad, weights.reshape(DOMAINS)


def build(mesh, nz, nx):
    placed = (P(("dp", "col"), "row"), P("row", "col"), P(("dp", "row"), "col"), P(), P(), P())
    return jax.shard_map(
        functools.partial(local, nz, nx, mesh.shape["row"], mesh.shape["col"]),
        mesh=mesh, in_specs=placed, out_specs=(P(("row", "dp"), "col"), P()), check_vma=False,
    )


def solution(mesh):
    return build(mesh, 8, mesh.shape["dp"] // 8)
```

```python
import functools

import jax
import jax.numpy as jnp
from jax import lax
from jax.experimental import pallas as pl
from jax.experimental.pallas import tpu as pltpu
from jax.sharding import PartitionSpec as P

DOMAINS = 16
SEQ = 128
PARTS = 4
FAR = 3
MESH = pl.DeviceIdType.MESH


def kernel(
    nz, nx, nr, nc,
    x_hbm, w_hbm, r_hbm, ref_hbm, label_hbm, prior_hbm,
    grad_ref, weights_ref,
    x_ref, w_ref, r_ref, ref_ref, label_ref, prior_ref,
    wbuf, rbuf, xt, tg, rowc, rowy, rowx, rowz, stage, got, send2, got2, far2, gotfar2, sum3, got3,
    xtp, rp, tgp, sump, gotp,
    in_s, wy_s, wy_r, w2_s, w2_r, r_s, r_r, f_s,
    c_s, c_r, y_s, y_r, x_s, x_r, z_s, z_r, p1_s, p1_r, p2_s, p2_r, p3_s, p3_r,
    pair_s, pair_r,
):
    tb, feat = x_ref.shape
    ob = w_ref.shape[-1]
    fb = feat // (nz * nx)
    hb = fb // 2
    sb = nc * ob // PARTS
    paired = nc == PARTS
    resp = tb // SEQ
    pairs_grp = nc * resp // 2
    all_pairs = label_ref.shape[1]
    per_col = ob // sb
    f32 = jnp.float32

    dp, row, col = lax.axis_index("dp"), lax.axis_index("row"), lax.axis_index("col")
    z, x = dp // nx, dp % nx
    cores = 2 if nr % 2 == 0 else 1
    y_high, core = row // cores, row % cores
    y, ny = y_high * nc + col, nr // cores * nc

    def at_core(k):
        return (dp, y_high * cores + lax.rem(core + k, cores), col)

    def at_y(k):
        other = lax.rem(y + k, ny)
        return (dp, other // nc * cores + core, other % nc)

    def at_x(k):
        return (z * nx + lax.rem(x + k, nx), row, col)

    def at_z(k):
        return (lax.rem(z + k, nz) * nx + x, row, col)

    def at_col(k):
        return (dp, row, lax.rem(col + k, nc))

    odd = col % 2
    pair = (dp, row, col + 1 - 2 * odd)

    def send(src, dst, ssem, rsem, dev):
        copy = pltpu.make_async_remote_copy(
            src_ref=src, dst_ref=dst, send_sem=ssem, recv_sem=rsem,
            device_id=dev, device_id_type=MESH,
        )
        copy.start()
        return copy

    sent = []
    axes = ((x, nx, at_x), (z, nz, at_z))

    loads = []
    for i, (src, dst) in enumerate((
        (w_hbm, w_ref), (r_hbm, r_ref), (x_hbm, x_ref),
        (label_hbm, label_ref), (ref_hbm, ref_ref), (prior_hbm, prior_ref),
    )):
        loads.append(pltpu.make_async_copy(src, dst, in_s.at[i]))
        loads[i].start()

    barrier = pltpu.get_barrier_semaphore()
    count = 0
    for n, at in ((cores, at_core), (ny, at_y), (nx, at_x), (nz, at_z)):
        for k in range(1, n):
            pl.semaphore_signal(barrier, inc=1, device_id=at(k), device_id_type=MESH)
            count += 1
    loads[0].wait()
    loads[1].wait()
    pl.semaphore_wait(barrier, count)

    lanes = (pl.ds(0, ob // 2), pl.ds(ob // 2, ob // 2))

    def w_block(ref, h, i):
        return ref.at[i, :, :, lanes[h]] if h == 0 else ref.at[:, i, :, lanes[h]]

    wy = []
    for k in range(1, nc):
        slot = nc - k - 1
        for h, i in enumerate((z, x)):
            wy.append(send(
                w_block(w_ref, h, i), w_block(wbuf.at[slot], h, i),
                wy_s.at[h, k], wy_r.at[h, slot], at_col(k),
            ))

    reads = []
    for k in range(1, nr // cores):
        there = lax.rem(y_high + k, nr // cores) * cores + core
        reads.append(send(r_ref, rbuf.at[col], r_s.at[k], r_r.at[col], (dp, there, row)))
    own_read = pltpu.make_async_copy(r_ref, rbuf.at[col], r_r.at[col])
    far_read = pltpu.make_async_remote_copy(
        src_ref=r_ref, dst_ref=rbuf.at[col], send_sem=r_s.at[0], recv_sem=r_r.at[col],
        device_id=(dp, row, row), device_id_type=MESH,
    )

    @pl.when(row == col)
    def _():
        own_read.start()

    @pl.when(row != col)
    def _():
        far_read.start()

    for load in loads[2:]:
        load.wait()
    for b in range(nz):
        block = x_ref[:, b * nx * fb:(b + 1) * nx * fb]
        block = jnp.swapaxes(block, 0, 1).reshape(nx, 2, hb, tb)
        xt[0, b] = block[:, 0]
        xt[1, b] = block[:, 1]
    lane = lax.broadcasted_iota(jnp.int32, (1, all_pairs), 1)
    onehot = (label_ref[...] == lax.broadcasted_iota(jnp.int32, (DOMAINS, all_pairs), 0)).astype(f32)
    counts = jnp.sum(onehot, axis=1, keepdims=True)

    chains, moving = [], {}
    for slot in range(nc - 1):
        for h in range(2):
            pos, n, at = axes[1 - h]
            for d, sign in enumerate((1, -1)):
                length = n // 2 if (h + slot + d) % 2 == 0 else n - 1 - n // 2
                chains.append((h, d, slot, pos, n, at, sign, length))

    def spread(s):
        for h, d, slot, pos, n, at, sign, length in chains:
            if s == 0 and d == 0:
                block = w_block(wbuf.at[slot], h, pos)
                pltpu.make_async_copy(block, block, wy_r.at[h, slot]).wait()
            if 0 < s <= length:
                moving[h, d, slot, s - 1].wait_recv()
            if s < length:
                block = w_block(wbuf.at[slot], h, lax.rem(pos - sign * s + n, n))
                moving[h, d, slot, s] = send(
                    block, block, w2_s.at[h, d, slot, s], w2_r.at[h, d, slot, s], at(sign % n)
                )

    if paired:
        sent.append(send(xt.at[0], xtp, pair_s.at[2], pair_r.at[2], pair))
    spread(0)

    passes = [
        pltpu.make_async_remote_copy(
            src_ref=rbuf.at[j], dst_ref=rbuf.at[j], send_sem=f_s.at[j], recv_sem=r_r.at[j],
            device_id=at_core(1), device_id_type=MESH,
        )
        for j in range(nc if cores > 1 else 0)
    ]
    passing = core == col % cores

    def pass_on():
        for j in range(nc):
            pltpu.make_async_copy(rbuf.at[j], rbuf.at[j], r_r.at[j]).wait()
            if cores > 1:
                @pl.when(passing)
                def _():
                    passes[j].start()

    steps = max(nx, nz) // 2
    def readout_ready():
        pass_on()
        if paired:
            for h in range(2):
                sent.append(send(rbuf.at[2 * h + 1 - odd], rp.at[h], pair_s.at[h], pair_r.at[h], pair))

    for s in range(1, steps):
        if s == max(steps - 1, 1):
            readout_ready()
        spread(s)
    if steps < 2:
        readout_ready()
    if steps > 0:
        spread(steps)
    sent += wy + list(moving.values())

    sums = [jnp.zeros((1, ob), f32) for _ in range(resp)]
    for k in range(nc):
        weight = (w_ref[...] if k == 0 else wbuf[k - 1]).reshape(feat, ob)
        values = jnp.dot(x_ref[...], weight, preferred_element_type=f32)
        prod = values * rbuf[lax.rem(col + k, nc)].astype(f32)
        for q in range(resp):
            sums[q] = sums[q] + jnp.sum(prod[q * SEQ:(q + 1) * SEQ], axis=0, keepdims=True)
    mine = jnp.zeros((1, all_pairs), f32)
    for q in range(resp):
        which = col * resp + q
        score = jnp.sum(sums[q], axis=1, keepdims=True)
        sign = jnp.where(which % 2 == 0, 1.0, -1.0).astype(f32)
        mine = mine + jnp.where(lane == dp * pairs_grp + which // 2, sign * score, 0.0)

    def exchange(buf, pos, n, at, ssem, rsem, value):
        buf[pos] = value
        copies = [send(buf.at[pos], buf.at[pos], ssem.at[k], rsem.at[k], at(k)) for k in range(1, n)]
        for copy in copies:
            copy.wait_recv()
        total = buf[0]
        for i in range(1, n):
            total = total + buf[i]
        sent.extend(copies)
        return total

    mine = exchange(rowc, core, cores, at_core, c_s, c_r, mine)
    mine = exchange(rowy, y, ny, at_y, y_s, y_r, mine)
    mine = exchange(rowx, x, nx, at_x, x_s, x_r, mine)
    mine = exchange(rowz, z, nz, at_z, z_s, z_r, mine)
    margin = mine - (ref_ref[0:1, :] - ref_ref[1:2, :])
    loss = jnp.maximum(-margin, 0.0) + jnp.log1p(jnp.exp(-jnp.abs(margin)))
    domain_loss = jnp.sum(onehot * loss, axis=1, keepdims=True) / counts
    eye = lax.broadcasted_iota(jnp.int32, (DOMAINS, DOMAINS), 0) == lax.broadcasted_iota(
        jnp.int32, (DOMAINS, DOMAINS), 1
    )
    prior = jnp.sum(jnp.where(eye, prior_ref[...], 0.0), axis=1, keepdims=True)
    raised = prior * jnp.exp(domain_loss)
    new_weights = raised / jnp.sum(raised, axis=0, keepdims=True)
    weights_ref[...] = jnp.sum(jnp.where(eye, new_weights, 0.0), axis=0, keepdims=True)
    coeff = (
        all_pairs * jax.nn.sigmoid(-margin)
        * jnp.sum(onehot * (new_weights / counts), axis=0, keepdims=True)
    )
    def scaled(column, q, block):
        which = column * resp + q
        own = jnp.sum(
            jnp.where(lane == dp * pairs_grp + which // 2, coeff, 0.0), axis=1, keepdims=True
        )
        own = own * jnp.where(which % 2 == 0, -1.0, 1.0).astype(f32)
        return (own * block.astype(f32)).astype(jnp.bfloat16)

    for q in range(resp):
        tokens = slice(q * SEQ, (q + 1) * SEQ)
        for j in range(PARTS):
            at_lane = (j % per_col) * sb
            tg[j, tokens, :] = scaled(col, q, rbuf[j // per_col, tokens, at_lane:at_lane + sb])

    def pair_ready():
        for i in range(3):
            there = rp.at[i] if i < 2 else xtp
            pltpu.make_async_copy(there, there, pair_r.at[i]).wait()
        for q in range(resp):
            tokens = slice(q * SEQ, (q + 1) * SEQ)
            for h in range(2):
                tgp[h, tokens, :] = scaled(pair[2], q, rp[h, tokens, :])

    if paired:
        units = ((1, 0, False), (1, 1, False), (0, 0, True))
    else:
        units = tuple((half, j, False) for half in range(2) for j in range(2))

    def part(h, target, unit):
        half, j, both = unit
        lhs = xt[half, :, target] if h == 0 else xt[half, target]
        lhs = lhs.reshape(lhs.shape[0] * hb, tb)
        if not both:
            return jnp.dot(lhs, tg[2 * h + j], preferred_element_type=f32)
        far = xtp[:, target] if h == 0 else xtp[target]
        return jnp.dot(lhs, tg[2 * h + odd], preferred_element_type=f32) + jnp.dot(
            far.reshape(lhs.shape), tgp[h], preferred_element_type=f32
        )

    chains = []
    for u in range(len(units)):
        for h in range(2):
            pos, n, at = axes[h]
            for d in range(2):
                length = n // 2 if (u + h + d) % 2 == 0 else n - 1 - n // 2
                chains.append((h, d, u, pos, n, at, 1 - 2 * d, length))
    moving = {}
    if paired and steps < 1:
        pair_ready()
    for s in range(steps):
        for h, d, u, pos, n, at, sign, length in chains:
            if s < length:
                if s == 0 and units[u][2] and (h, d) == (0, 0):
                    pair_ready()
                chunk = part(h, lax.rem(pos + sign * (length - s) + n, n), units[u])
                if s > 0:
                    moving[h, d, u, s - 1].wait_recv()
                    chunk = chunk + got[h, d, u, s - 1].astype(f32)
                stage[h, d, u, s] = chunk.astype(jnp.bfloat16)
                moving[h, d, u, s] = send(
                    stage.at[h, d, u, s], got.at[h, d, u, s],
                    p1_s.at[h, d, u, s], p1_r.at[h, d, u, s], at(sign % n),
                )
    for u in range(len(units)):
        for h in range(2):
            pos, n, at = axes[h]
            chunk = part(h, pos, units[u])
            for ch in chains:
                if ch[0] == h and ch[2] == u and ch[7] > 0:
                    last = ch[7] - 1
                    moving[h, ch[1], u, last].wait_recv()
                    chunk = chunk + got[h, ch[1], u, last].astype(f32)
            send2[h, :, u] = chunk.reshape(n, hb, sb)
    sent += list(moving.values())

    second = []
    for h in range(2):
        pos, n, at = axes[1 - h]
        for k in sorted(range(1, n), key=lambda k: -min(k, n - k)):
            target, src, dst = lax.rem(pos + k, n), send2, got2
            if min(k, n - k) >= FAR:
                far2[h, target] = send2[h, target].astype(jnp.bfloat16)
                src, dst = far2, gotfar2
            second.append(send(
                src.at[h, target], dst.at[h, pos], p2_s.at[h, k], p2_r.at[h, k], at(k)
            ))
    for copy in second:
        copy.wait_recv()
    sent += second
    for h in range(2):
        pos, n, at = axes[1 - h]
        total = send2[h, pos]
        for k in range(1, n):
            there = gotfar2 if min(k, n - k) >= FAR else got2
            total = total + there[h, lax.rem(pos - k + n, n)].astype(f32)
        for u, (half, j, both) in enumerate(units):
            if both:
                sump[h] = total[u]
            else:
                sum3[2 * h + j, 0 if paired else half] = total[u]

    third = []
    for k in range(1, nc):
        target = lax.rem(col + k, nc)
        third.append(send(
            sum3.at[pl.ds(target * per_col, per_col)], got3.at[col], p3_s.at[k], p3_r.at[k], at_col(k)
        ))
    if paired:
        third.append(send(sump.at[1 - col // 2], gotp, pair_s.at[3], pair_r.at[3], at_col(2)))
    for copy in third:
        copy.wait_recv()
    sent += third
    for i in range(per_col):
        total = sum3[col * per_col + i]
        for k in range(1, nc):
            total = total + got3[lax.rem(col - k + nc, nc), i]
        at_lane = slice(i * sb, (i + 1) * sb)
        if paired:
            grad_ref[hb:, at_lane] = total[0]
            grad_ref[:hb, at_lane] = sump[col // 2] + gotp[...]
        else:
            grad_ref[:, at_lane] = total.reshape(fb, sb)

    for copy in reads + sent:
        copy.wait_send()

    @pl.when(row != col)
    def _():
        far_read.wait_send()

    if cores > 1:
        @pl.when(passing)
        def _():
            for copy in passes:
                copy.wait_send()


def local(nz, nx, nr, nc, attn_mix, value_weight, readout, ref_scores, domain_label, prior_weights):
    tb, feat = attn_mix.shape
    ob = value_weight.shape[1]
    fb = feat // (nz * nx)
    sb = nc * ob // PARTS
    all_pairs = domain_label.shape[0]
    ring = max(nz, nx)
    hb = fb // 2
    paired = nc == PARTS
    units = 3 if paired else 4
    cores = 2 if nr % 2 == 0 else 1
    ny = nr // cores * nc
    vmem = pl.BlockSpec(memory_space=pltpu.VMEM)
    bf16, f32 = jnp.bfloat16, jnp.float32
    dma = pltpu.SemaphoreType.DMA
    assert nz == nx
    grad, weights = pl.pallas_call(
        functools.partial(kernel, nz, nx, nr, nc),
        out_shape=(
            jax.ShapeDtypeStruct((fb, ob), f32),
            jax.ShapeDtypeStruct((1, DOMAINS), f32),
        ),
        in_specs=[pl.BlockSpec(memory_space=pl.ANY)] * 6,
        out_specs=(vmem, vmem),
        scratch_shapes=[
            pltpu.VMEM(attn_mix.shape, bf16),
            pltpu.VMEM((nz, nx, fb, ob), bf16),
            pltpu.VMEM(readout.shape, bf16),
            pltpu.VMEM((2, all_pairs), f32),
            pltpu.VMEM((1, all_pairs), jnp.int32),
            pltpu.VMEM((1, DOMAINS), f32),
            pltpu.VMEM((max(nc - 1, 1), nz, nx, fb, ob), bf16),
            pltpu.VMEM((nc, tb, ob), bf16),
            pltpu.VMEM((2, nz, nx, hb, tb), bf16),
            pltpu.VMEM((PARTS, tb, sb), bf16),
            pltpu.VMEM((cores, 1, all_pairs), f32),
            pltpu.VMEM((ny, 1, all_pairs), f32),
            pltpu.VMEM((nx, 1, all_pairs), f32),
            pltpu.VMEM((nz, 1, all_pairs), f32),
            pltpu.VMEM((2, 2, 4, max(ring // 2, 1), ring * hb, sb), bf16),
            pltpu.VMEM((2, 2, 4, max(ring // 2, 1), ring * hb, sb), bf16),
            pltpu.VMEM((2, ring, units, hb, sb), f32),
            pltpu.VMEM((2, ring, units, hb, sb), f32),
            pltpu.VMEM((2, ring, units, hb, sb), bf16),
            pltpu.VMEM((2, ring, units, hb, sb), bf16),
            pltpu.VMEM((PARTS, 1 if paired else 2, hb, sb), f32),
            pltpu.VMEM((nc, ob // sb, 1 if paired else 2, hb, sb), f32),
            pltpu.VMEM((nz, nx, hb, tb), bf16),
            pltpu.VMEM((2, tb, sb), bf16),
            pltpu.VMEM((2, tb, sb), bf16),
            pltpu.VMEM((2, hb, sb), f32),
            pltpu.VMEM((hb, sb), f32),
            dma((6,)),
            dma((2, nc)), dma((2, nc)),
            dma((2, 2, max(nc - 1, 1), max(ring // 2, 1))), dma((2, 2, max(nc - 1, 1), max(ring // 2, 1))),
            dma((nr,)), dma((nc,)), dma((nc,)),
            dma((cores,)), dma((cores,)),
            dma((ny,)), dma((ny,)),
            dma((nx,)), dma((nx,)),
            dma((nz,)), dma((nz,)),
            dma((2, 2, 4, max(ring // 2, 1))), dma((2, 2, 4, max(ring // 2, 1))),
            dma((2, ring)), dma((2, ring)),
            dma((nc,)), dma((nc,)),
            dma((4,)), dma((4,)),
        ],
        compiler_params=pltpu.CompilerParams(
            collective_id=0, has_side_effects=True, vmem_limit_bytes=56 * 1024 * 1024
        ),
        cost_estimate=pl.CostEstimate(
            flops=4 * tb * feat * nc * ob, bytes_accessed=4 * tb * feat, transcendentals=0
        ),
    )(
        attn_mix, value_weight.reshape(nz, nx, fb, ob), readout,
        ref_scores.T, domain_label.T, prior_weights.reshape(1, DOMAINS),
    )
    return grad, weights.reshape(DOMAINS)


def build(mesh, nz, nx):
    placed = (P(("dp", "col"), "row"), P("row", "col"), P(("dp", "row"), "col"), P(), P(), P())
    return jax.shard_map(
        functools.partial(local, nz, nx, mesh.shape["row"], mesh.shape["col"]),
        mesh=mesh, in_specs=placed, out_specs=(P(("row", "dp"), "col"), P()), check_vma=False,
    )


def solution(mesh):
    return build(mesh, 8, mesh.shape["dp"] // 8)
```

```python
import functools

import jax
import jax.numpy as jnp
from jax import lax
from jax.experimental import pallas as pl
from jax.experimental.pallas import tpu as pltpu
from jax.sharding import PartitionSpec as P

DOMAINS = 16
SEQ = 128
PARTS = 4
FAR = 3
MESH = pl.DeviceIdType.MESH


def kernel(
    nz, nx, nr, nc,
    x_hbm, w_hbm, r_hbm, ref_hbm, label_hbm, prior_hbm,
    grad_ref, weights_ref,
    x_ref, w_ref, r_ref, ref_ref, label_ref, prior_ref,
    wbuf, rbuf, xt, tg, rowc, rowy, rowx, rowz, stage, got, send2, got2, far2, gotfar2, sum3, got3,
    xtp, rp, tgp, sump, gotp,
    in_s, wy_s, wy_r, w2_s, w2_r, r_s, r_r, f_s,
    c_s, c_r, y_s, y_r, x_s, x_r, z_s, z_r, p1_s, p1_r, p2_s, p2_r, p3_s, p3_r,
    pair_s, pair_r,
):
    tb, feat = x_ref.shape
    ob = w_ref.shape[-1]
    fb = feat // (nz * nx)
    hb = fb // 2
    sb = nc * ob // PARTS
    paired = nc == PARTS
    resp = tb // SEQ
    pairs_grp = nc * resp // 2
    all_pairs = label_ref.shape[1]
    per_col = ob // sb
    f32 = jnp.float32

    dp, row, col = lax.axis_index("dp"), lax.axis_index("row"), lax.axis_index("col")
    z, x = dp // nx, dp % nx
    cores = 2 if nr % 2 == 0 else 1
    y_high, core = row // cores, row % cores
    y, ny = y_high * nc + col, nr // cores * nc

    def at_core(k):
        return (dp, y_high * cores + lax.rem(core + k, cores), col)

    def at_y(k):
        other = lax.rem(y + k, ny)
        return (dp, other // nc * cores + core, other % nc)

    def at_x(k):
        return (z * nx + lax.rem(x + k, nx), row, col)

    def at_z(k):
        return (lax.rem(z + k, nz) * nx + x, row, col)

    def at_col(k):
        return (dp, row, lax.rem(col + k, nc))

    odd = col % 2
    pair = (dp, row, col + 1 - 2 * odd)

    def send(src, dst, ssem, rsem, dev):
        copy = pltpu.make_async_remote_copy(
            src_ref=src, dst_ref=dst, send_sem=ssem, recv_sem=rsem,
            device_id=dev, device_id_type=MESH,
        )
        copy.start()
        return copy

    sent = []
    axes = ((x, nx, at_x), (z, nz, at_z))

    loads = []
    for i, (src, dst) in enumerate((
        (w_hbm, w_ref), (r_hbm, r_ref), (x_hbm, x_ref),
        (label_hbm, label_ref), (ref_hbm, ref_ref), (prior_hbm, prior_ref),
    )):
        loads.append(pltpu.make_async_copy(src, dst, in_s.at[i]))
        loads[i].start()

    barrier = pltpu.get_barrier_semaphore()
    count = 0
    for n, at in ((cores, at_core), (ny, at_y), (nx, at_x), (nz, at_z)):
        for k in range(1, n):
            pl.semaphore_signal(barrier, inc=1, device_id=at(k), device_id_type=MESH)
            count += 1
    loads[0].wait()
    loads[1].wait()
    pl.semaphore_wait(barrier, count)

    lanes = (pl.ds(0, ob // 2), pl.ds(ob // 2, ob // 2))

    def w_block(ref, h, i):
        return ref.at[i, :, :, lanes[h]] if h == 0 else ref.at[:, i, :, lanes[h]]

    wy = []
    for k in range(1, nc):
        slot = nc - k - 1
        for h, i in enumerate((z, x)):
            wy.append(send(
                w_block(w_ref, h, i), w_block(wbuf.at[slot], h, i),
                wy_s.at[h, k], wy_r.at[h, slot], at_col(k),
            ))

    reads = []
    for k in range(1, nr // cores):
        there = lax.rem(y_high + k, nr // cores) * cores + core
        reads.append(send(r_ref, rbuf.at[col], r_s.at[k], r_r.at[col], (dp, there, row)))
    own_read = pltpu.make_async_copy(r_ref, rbuf.at[col], r_r.at[col])
    far_read = pltpu.make_async_remote_copy(
        src_ref=r_ref, dst_ref=rbuf.at[col], send_sem=r_s.at[0], recv_sem=r_r.at[col],
        device_id=(dp, row, row), device_id_type=MESH,
    )

    @pl.when(row == col)
    def _():
        own_read.start()

    @pl.when(row != col)
    def _():
        far_read.start()

    for load in loads[2:]:
        load.wait()
    for b in range(nz):
        block = x_ref[:, b * nx * fb:(b + 1) * nx * fb]
        block = jnp.swapaxes(block, 0, 1).reshape(nx, 2, hb, tb)
        xt[0, b] = block[:, 0]
        xt[1, b] = block[:, 1]
    lane = lax.broadcasted_iota(jnp.int32, (1, all_pairs), 1)
    onehot = (label_ref[...] == lax.broadcasted_iota(jnp.int32, (DOMAINS, all_pairs), 0)).astype(f32)
    counts = jnp.sum(onehot, axis=1, keepdims=True)

    chains, moving = [], {}
    for slot in range(nc - 1):
        for h in range(2):
            pos, n, at = axes[1 - h]
            for d, sign in enumerate((1, -1)):
                length = n // 2 if (h + slot + d) % 2 == 0 else n - 1 - n // 2
                chains.append((h, d, slot, pos, n, at, sign, length))

    def spread(s):
        for h, d, slot, pos, n, at, sign, length in chains:
            if s == 0 and d == 0:
                block = w_block(wbuf.at[slot], h, pos)
                pltpu.make_async_copy(block, block, wy_r.at[h, slot]).wait()
            if 0 < s <= length:
                moving[h, d, slot, s - 1].wait_recv()
            if s < length:
                block = w_block(wbuf.at[slot], h, lax.rem(pos - sign * s + n, n))
                moving[h, d, slot, s] = send(
                    block, block, w2_s.at[h, d, slot, s], w2_r.at[h, d, slot, s], at(sign % n)
                )

    if paired:
        sent.append(send(xt.at[0], xtp, pair_s.at[2], pair_r.at[2], pair))
    spread(0)

    passes = [
        pltpu.make_async_remote_copy(
            src_ref=rbuf.at[j], dst_ref=rbuf.at[j], send_sem=f_s.at[j], recv_sem=r_r.at[j],
            device_id=at_core(1), device_id_type=MESH,
        )
        for j in range(nc if cores > 1 else 0)
    ]
    passing = core == col % cores

    def pass_on():
        for j in range(nc):
            pltpu.make_async_copy(rbuf.at[j], rbuf.at[j], r_r.at[j]).wait()
            if cores > 1:
                @pl.when(passing)
                def _():
                    passes[j].start()

    steps = max(nx, nz) // 2
    def add_scores(k):
        weight = (w_ref[...] if k == 0 else wbuf[k - 1]).reshape(feat, ob)
        values = jnp.dot(x_ref[...], weight, preferred_element_type=f32)
        prod = values * rbuf[lax.rem(col + k, nc)].astype(f32)
        for q in range(resp):
            sums[q] = sums[q] + jnp.sum(prod[q * SEQ:(q + 1) * SEQ], axis=0, keepdims=True)

    def readout_ready():
        pass_on()
        if paired:
            for h in range(2):
                sent.append(send(rbuf.at[2 * h + 1 - odd], rp.at[h], pair_s.at[h], pair_r.at[h], pair))

    for s in range(1, steps):
        if s == max(steps - 1, 1):
            readout_ready()
        spread(s)
    if steps < 2:
        readout_ready()
    sums = [jnp.zeros((1, ob), f32) for _ in range(resp)]
    add_scores(0)
    if steps > 0:
        spread(steps)
    sent += wy + list(moving.values())

    for k in range(1, nc):
        add_scores(k)
    mine = jnp.zeros((1, all_pairs), f32)
    for q in range(resp):
        which = col * resp + q
        score = jnp.sum(sums[q], axis=1, keepdims=True)
        sign = jnp.where(which % 2 == 0, 1.0, -1.0).astype(f32)
        mine = mine + jnp.where(lane == dp * pairs_grp + which // 2, sign * score, 0.0)

    def exchange(buf, pos, n, at, ssem, rsem, value):
        buf[pos] = value
        copies = [send(buf.at[pos], buf.at[pos], ssem.at[k], rsem.at[k], at(k)) for k in range(1, n)]
        for copy in copies:
            copy.wait_recv()
        total = buf[0]
        for i in range(1, n):
            total = total + buf[i]
        sent.extend(copies)
        return total

    mine = exchange(rowc, core, cores, at_core, c_s, c_r, mine)
    mine = exchange(rowy, y, ny, at_y, y_s, y_r, mine)
    mine = exchange(rowx, x, nx, at_x, x_s, x_r, mine)
    mine = exchange(rowz, z, nz, at_z, z_s, z_r, mine)
    margin = mine - (ref_ref[0:1, :] - ref_ref[1:2, :])
    loss = jnp.maximum(-margin, 0.0) + jnp.log1p(jnp.exp(-jnp.abs(margin)))
    domain_loss = jnp.sum(onehot * loss, axis=1, keepdims=True) / counts
    eye = lax.broadcasted_iota(jnp.int32, (DOMAINS, DOMAINS), 0) == lax.broadcasted_iota(
        jnp.int32, (DOMAINS, DOMAINS), 1
    )
    prior = jnp.sum(jnp.where(eye, prior_ref[...], 0.0), axis=1, keepdims=True)
    raised = prior * jnp.exp(domain_loss)
    new_weights = raised / jnp.sum(raised, axis=0, keepdims=True)
    weights_ref[...] = jnp.sum(jnp.where(eye, new_weights, 0.0), axis=0, keepdims=True)
    coeff = (
        all_pairs * jax.nn.sigmoid(-margin)
        * jnp.sum(onehot * (new_weights / counts), axis=0, keepdims=True)
    )
    def scaled(column, q, block):
        which = column * resp + q
        own = jnp.sum(
            jnp.where(lane == dp * pairs_grp + which // 2, coeff, 0.0), axis=1, keepdims=True
        )
        own = own * jnp.where(which % 2 == 0, -1.0, 1.0).astype(f32)
        return (own * block.astype(f32)).astype(jnp.bfloat16)

    for q in range(resp):
        tokens = slice(q * SEQ, (q + 1) * SEQ)
        for j in range(PARTS):
            at_lane = (j % per_col) * sb
            tg[j, tokens, :] = scaled(col, q, rbuf[j // per_col, tokens, at_lane:at_lane + sb])

    def pair_ready():
        for i in range(3):
            there = rp.at[i] if i < 2 else xtp
            pltpu.make_async_copy(there, there, pair_r.at[i]).wait()
        for q in range(resp):
            tokens = slice(q * SEQ, (q + 1) * SEQ)
            for h in range(2):
                tgp[h, tokens, :] = scaled(pair[2], q, rp[h, tokens, :])

    if paired:
        units = ((1, 0, False), (1, 1, False), (0, 0, True))
    else:
        units = tuple((half, j, False) for half in range(2) for j in range(2))

    def part(h, target, unit):
        half, j, both = unit
        lhs = xt[half, :, target] if h == 0 else xt[half, target]
        lhs = lhs.reshape(lhs.shape[0] * hb, tb)
        if not both:
            return jnp.dot(lhs, tg[2 * h + j], preferred_element_type=f32)
        far = xtp[:, target] if h == 0 else xtp[target]
        return jnp.dot(lhs, tg[2 * h + odd], preferred_element_type=f32) + jnp.dot(
            far.reshape(lhs.shape), tgp[h], preferred_element_type=f32
        )

    chains = []
    for u in range(len(units)):
        for h in range(2):
            pos, n, at = axes[h]
            for d in range(2):
                length = n // 2 if (u + h + d) % 2 == 0 else n - 1 - n // 2
                chains.append((h, d, u, pos, n, at, 1 - 2 * d, length))
    moving = {}
    if paired and steps < 1:
        pair_ready()
    for s in range(steps):
        for h, d, u, pos, n, at, sign, length in chains:
            if s < length:
                if s == 0 and units[u][2] and (h, d) == (0, 0):
                    pair_ready()
                chunk = part(h, lax.rem(pos + sign * (length - s) + n, n), units[u])
                if s > 0:
                    moving[h, d, u, s - 1].wait_recv()
                    chunk = chunk + got[h, d, u, s - 1].astype(f32)
                stage[h, d, u, s] = chunk.astype(jnp.bfloat16)
                moving[h, d, u, s] = send(
                    stage.at[h, d, u, s], got.at[h, d, u, s],
                    p1_s.at[h, d, u, s], p1_r.at[h, d, u, s], at(sign % n),
                )
    second = []

    def second_phase(h):
        pos, n, at = axes[1 - h]
        for k in sorted(range(1, n), key=lambda k: -min(k, n - k)):
            target, src, dst = lax.rem(pos + k, n), send2, got2
            if min(k, n - k) >= FAR:
                far2[h, target] = send2[h, target].astype(jnp.bfloat16)
                src, dst = far2, gotfar2
            second.append(send(
                src.at[h, target], dst.at[h, pos], p2_s.at[h, k], p2_r.at[h, k], at(k)
            ))

    for h in range(2):
        pos, n, at = axes[h]
        for u in range(len(units)):
            chunk = part(h, pos, units[u])
            for ch in chains:
                if ch[0] == h and ch[2] == u and ch[7] > 0:
                    last = ch[7] - 1
                    moving[h, ch[1], u, last].wait_recv()
                    chunk = chunk + got[h, ch[1], u, last].astype(f32)
            send2[h, :, u] = chunk.reshape(n, hb, sb)
        second_phase(h)
    sent += list(moving.values())

    for copy in second:
        copy.wait_recv()
    sent += second
    for h in range(2):
        pos, n, at = axes[1 - h]
        total = send2[h, pos]
        for k in range(1, n):
            there = gotfar2 if min(k, n - k) >= FAR else got2
            total = total + there[h, lax.rem(pos - k + n, n)].astype(f32)
        for u, (half, j, both) in enumerate(units):
            if both:
                sump[h] = total[u]
            else:
                sum3[2 * h + j, 0 if paired else half] = total[u]

    third = []
    for k in range(1, nc):
        target = lax.rem(col + k, nc)
        third.append(send(
            sum3.at[pl.ds(target * per_col, per_col)], got3.at[col], p3_s.at[k], p3_r.at[k], at_col(k)
        ))
    if paired:
        third.append(send(sump.at[1 - col // 2], gotp, pair_s.at[3], pair_r.at[3], at_col(2)))
    for copy in third:
        copy.wait_recv()
    sent += third
    for i in range(per_col):
        total = sum3[col * per_col + i]
        for k in range(1, nc):
            total = total + got3[lax.rem(col - k + nc, nc), i]
        at_lane = slice(i * sb, (i + 1) * sb)
        if paired:
            grad_ref[hb:, at_lane] = total[0]
            grad_ref[:hb, at_lane] = sump[col // 2] + gotp[...]
        else:
            grad_ref[:, at_lane] = total.reshape(fb, sb)

    for copy in reads + sent:
        copy.wait_send()

    @pl.when(row != col)
    def _():
        far_read.wait_send()

    if cores > 1:
        @pl.when(passing)
        def _():
            for copy in passes:
                copy.wait_send()


def local(nz, nx, nr, nc, attn_mix, value_weight, readout, ref_scores, domain_label, prior_weights):
    tb, feat = attn_mix.shape
    ob = value_weight.shape[1]
    fb = feat // (nz * nx)
    sb = nc * ob // PARTS
    all_pairs = domain_label.shape[0]
    ring = max(nz, nx)
    hb = fb // 2
    paired = nc == PARTS
    units = 3 if paired else 4
    cores = 2 if nr % 2 == 0 else 1
    ny = nr // cores * nc
    vmem = pl.BlockSpec(memory_space=pltpu.VMEM)
    bf16, f32 = jnp.bfloat16, jnp.float32
    dma = pltpu.SemaphoreType.DMA
    assert nz == nx
    grad, weights = pl.pallas_call(
        functools.partial(kernel, nz, nx, nr, nc),
        out_shape=(
            jax.ShapeDtypeStruct((fb, ob), f32),
            jax.ShapeDtypeStruct((1, DOMAINS), f32),
        ),
        in_specs=[pl.BlockSpec(memory_space=pl.ANY)] * 6,
        out_specs=(vmem, vmem),
        scratch_shapes=[
            pltpu.VMEM(attn_mix.shape, bf16),
            pltpu.VMEM((nz, nx, fb, ob), bf16),
            pltpu.VMEM(readout.shape, bf16),
            pltpu.VMEM((2, all_pairs), f32),
            pltpu.VMEM((1, all_pairs), jnp.int32),
            pltpu.VMEM((1, DOMAINS), f32),
            pltpu.VMEM((max(nc - 1, 1), nz, nx, fb, ob), bf16),
            pltpu.VMEM((nc, tb, ob), bf16),
            pltpu.VMEM((2, nz, nx, hb, tb), bf16),
            pltpu.VMEM((PARTS, tb, sb), bf16),
            pltpu.VMEM((cores, 1, all_pairs), f32),
            pltpu.VMEM((ny, 1, all_pairs), f32),
            pltpu.VMEM((nx, 1, all_pairs), f32),
            pltpu.VMEM((nz, 1, all_pairs), f32),
            pltpu.VMEM((2, 2, 4, max(ring // 2, 1), ring * hb, sb), bf16),
            pltpu.VMEM((2, 2, 4, max(ring // 2, 1), ring * hb, sb), bf16),
            pltpu.VMEM((2, ring, units, hb, sb), f32),
            pltpu.VMEM((2, ring, units, hb, sb), f32),
            pltpu.VMEM((2, ring, units, hb, sb), bf16),
            pltpu.VMEM((2, ring, units, hb, sb), bf16),
            pltpu.VMEM((PARTS, 1 if paired else 2, hb, sb), f32),
            pltpu.VMEM((nc, ob // sb, 1 if paired else 2, hb, sb), f32),
            pltpu.VMEM((nz, nx, hb, tb), bf16),
            pltpu.VMEM((2, tb, sb), bf16),
            pltpu.VMEM((2, tb, sb), bf16),
            pltpu.VMEM((2, hb, sb), f32),
            pltpu.VMEM((hb, sb), f32),
            dma((6,)),
            dma((2, nc)), dma((2, nc)),
            dma((2, 2, max(nc - 1, 1), max(ring // 2, 1))), dma((2, 2, max(nc - 1, 1), max(ring // 2, 1))),
            dma((nr,)), dma((nc,)), dma((nc,)),
            dma((cores,)), dma((cores,)),
            dma((ny,)), dma((ny,)),
            dma((nx,)), dma((nx,)),
            dma((nz,)), dma((nz,)),
            dma((2, 2, 4, max(ring // 2, 1))), dma((2, 2, 4, max(ring // 2, 1))),
            dma((2, ring)), dma((2, ring)),
            dma((nc,)), dma((nc,)),
            dma((4,)), dma((4,)),
        ],
        compiler_params=pltpu.CompilerParams(
            collective_id=0, has_side_effects=True, vmem_limit_bytes=56 * 1024 * 1024
        ),
        cost_estimate=pl.CostEstimate(
            flops=4 * tb * feat * nc * ob, bytes_accessed=4 * tb * feat, transcendentals=0
        ),
    )(
        attn_mix, value_weight.reshape(nz, nx, fb, ob), readout,
        ref_scores.T, domain_label.T, prior_weights.reshape(1, DOMAINS),
    )
    return grad, weights.reshape(DOMAINS)


def build(mesh, nz, nx):
    placed = (P(("dp", "col"), "row"), P("row", "col"), P(("dp", "row"), "col"), P(), P(), P())
    return jax.shard_map(
        functools.partial(local, nz, nx, mesh.shape["row"], mesh.shape["col"]),
        mesh=mesh, in_specs=placed, out_specs=(P(("row", "dp"), "col"), P()), check_vma=False,
    )


def solution(mesh):
    return build(mesh, 8, mesh.shape["dp"] // 8)
```
